256 devices in a mesh: blk: 32 (over z_lo, y, core), col: 2 (over z_hi), rep: 4 (over x).
Axes of the slice: x: 4, y: 4, z: 8 (z_hi: 2, z_lo: 4; z = z_hi * 4 + z_lo), core: 2. Of those that a mesh axis runs over, the one named last changes fastest.
Arguments:
- feats: bfloat16 [65536, 256], P('blk', 'col'), may hold values from -6 to 6
- agg_feats: bfloat16 [65536, 256], P('blk', 'col'), may hold values from -6 to 6
- grad_out: bfloat16 [65536, 256], P('blk', 'col'), may hold values from -6 to 6
- w_self: bfloat16 [256, 256], P('col'), may hold values from -0.375 to 0.375
- w_neigh: bfloat16 [256, 256], P('col'), may hold values from -0.375 to 0.375
- degree: int32 [65536], P('blk'), may hold values from 1 to 64
- tile_vals: bfloat16 [32, 32, 40, 128, 128], P('blk', 'rep'), may hold values from 0 to 1
- tile_rows: int32 [32, 32, 40], P('blk', 'rep'), may hold values from 0 to 15
- tile_cols: int32 [32, 32, 40], P('blk', 'rep'), may hold values from 0 to 15
- tile_count: int32 [32, 32], P('blk', 'rep'), may hold values from 0 to 40, as said below
Outputs:
- grad_feats: bfloat16 [65536, 256], P('blk', 'col')
- grad_weight: float32 [2, 256, 256], P(None, 'col')
The draws below stay inside these ranges and needn't reach their ends.
Inputs may be any that keep to these rules, and one draw needn't show every extreme that they name: `tile_count`: the tile slots of a pair at or past its count hold tiles that are not part of the graph.
All inputs are finite; a program needn't handle non-finite values.
Results may differ from the reference program's by a relative error of at most 0.0049.
Values may be sent and summed in bfloat16 or wider, within the bound.
No kernel may reach another device: no remote copies, remote signals or barrier semaphores. Data moves between devices by JAX's collectives and lax.ppermute only.
A program may use at most 128 MiB of HBM per device.

```python
import math
import jax
import jax.numpy as jnp
from jax import lax

FIN = 256
FOUT = 256
TILE = 128
NT_DEV = 16
MAXT = 40
BLOCKS = 32
NODES = 65536


def draw_tile_count(key, part):
    key = jax.random.fold_in(key, 11)
    first_key, second_key, spot_key = jax.random.split(key, 3)
    left_level = jax.random.randint(first_key, (BLOCKS, BLOCKS), 0, MAXT + 1)
    right_level = jax.random.randint(second_key, (BLOCKS, BLOCKS), 0, MAXT + 1)
    counts = (left_level * right_level // MAXT).reshape(-1)
    spot = jax.random.randint(spot_key, (), 0, BLOCKS * BLOCKS)
    counts = jnp.where(jnp.arange(BLOCKS * BLOCKS) == spot, MAXT, counts)
    return counts.reshape(BLOCKS, BLOCKS).astype(jnp.int32)


def set_ends(array, rng, low, largest):
    index_at = [jax.random.randint(jax.random.fold_in(rng, axis), (), 0, length) for axis, length in enumerate(array.shape)]
    longest = array.shape.index(max(array.shape))
    beside = index_at[:longest] + [(index_at[longest] + 1) % array.shape[longest]] + index_at[longest + 1:]
    return array.at[tuple(index_at)].set(low).at[tuple(beside)].set(largest)


def block_levels(rng, shape, shards, least, largest):
    def one(axis_at, blocks):
        heights = jax.random.uniform(jax.random.fold_in(jax.random.fold_in(rng, 6), axis_at), (blocks,), jnp.float32, least / len(shards), largest / len(shards))
        return jnp.repeat(jnp.exp(heights), shape[axis_at] // blocks).reshape((-1,) + (1,) * (len(shape) - axis_at - 1))

    level = one(*shards[0])
    for cut in shards[1:]:
        level = level * one(*cut)
    return level


def noise(key, dims, deviation, limit, pieces=(), kind=jnp.bfloat16):
    drawn = deviation * jax.random.normal(key, dims, jnp.float32)
    if pieces:
        drawn = drawn * block_levels(key, dims, pieces, -0.22, 0.18)
    return jnp.clip(drawn, -limit, limit).astype(kind)


def setup_inputs(seed: int = 0) -> dict:
    keys = jax.random.split(jax.random.key(seed), 11)
    return {
        "feats": noise(keys[0], (NODES, FIN), 1.0, 6.0, ((0, 32), (1, 2))),
        "agg_feats": noise(keys[1], (NODES, FIN), 1.0, 6.0, ((0, 32), (1, 2))),
        "grad_out": noise(keys[2], (NODES, FOUT), 1.0, 6.0, ((0, 32), (1, 2))),
        "w_self": noise(keys[3], (FIN, FOUT), FIN ** -0.5, 0.375, ((0, 2),)),
        "w_neigh": noise(keys[4], (FIN, FOUT), FIN ** -0.5, 0.375, ((0, 2),)),
        "degree": set_ends(jax.random.randint(keys[5], (NODES,), 1, 65), jax.random.fold_in(keys[5], 1), 1, 64).astype(jnp.int32),
        "tile_vals": jnp.clip(1.0 * jax.random.uniform(keys[6], (BLOCKS, BLOCKS, MAXT, TILE, TILE), jnp.float32) ** block_levels(keys[6], (BLOCKS, BLOCKS, MAXT, TILE, TILE), ((0, 32), (1, 4)), -0.2, 0.2), 0.0, 1.0).astype(jnp.bfloat16),
        "tile_rows": set_ends(jax.random.randint(keys[7], (BLOCKS, BLOCKS, MAXT), 0, NT_DEV), jax.random.fold_in(keys[7], 1), 0, NT_DEV - 1).astype(jnp.int32),
        "tile_cols": set_ends(jax.random.randint(keys[8], (BLOCKS, BLOCKS, MAXT), 0, NT_DEV), jax.random.fold_in(keys[8], 1), 0, NT_DEV - 1).astype(jnp.int32),
        "tile_count": draw_tile_count(jax.random.fold_in(keys[10], 71), 0),
    }


def reference(feats, agg_feats, grad_out, w_self, w_neigh, degree, tile_vals, tile_rows, tile_cols, tile_count):
    scaled = (jnp.dot(grad_out, w_neigh.T, preferred_element_type=jnp.float32) / degree.astype(jnp.float32)[:, None]).astype(jnp.bfloat16)
    panels = scaled.reshape(BLOCKS, NT_DEV, TILE, FIN)
    slot_index = jnp.arange(MAXT)

    def per_owner(owner):

        def per_distance(running, distance):
            source = (owner - distance) % BLOCKS
            picked = panels[source][tile_rows[owner, distance]].astype(jnp.float32)
            edge_values = tile_vals[owner, distance].astype(jnp.float32)
            product = jnp.einsum('tab,taf->tbf', edge_values, picked)
            live_mask = slot_index < tile_count[owner, distance]
            product = jnp.where(live_mask[:, None, None], product, jnp.zeros_like(product))
            return (running.at[tile_cols[owner, distance]].add(product), None)
        running, _ = lax.scan(per_distance, jnp.zeros((NT_DEV, TILE, FIN), jnp.float32), jnp.arange(BLOCKS))
        return running
    neighbour_grad = lax.map(per_owner, jnp.arange(BLOCKS)).reshape(NODES, FIN)
    self_term = jnp.dot(grad_out, w_self.T, preferred_element_type=jnp.float32)
    grad_feats = (self_term + neighbour_grad).astype(jnp.bfloat16)
    grad_weight = jnp.stack([jnp.dot(feats.T, grad_out, preferred_element_type=jnp.float32), jnp.dot(agg_feats.T, grad_out, preferred_element_type=jnp.float32)])
    grad_weight = grad_weight * (1.0 / math.sqrt(NODES))
    return (grad_feats, grad_weight)
```

```python
import functools
import math

import jax
import jax.numpy as jnp
from jax import lax
from jax.experimental import pallas as pl
from jax.experimental.pallas import tpu as pltpu
from jax.sharding import PartitionSpec as P

NZ, NY, NC, NR = 4, 4, 2, 4
BLK = NZ * NY * NC
TILE = 128
NT = 16
HALF = 64
BF = jnp.bfloat16
F32 = jnp.float32
VMEM = pl.BlockSpec(memory_space=pltpu.VMEM)
SMEM = pl.BlockSpec(memory_space=pltpu.SMEM)
ANY = pl.BlockSpec(memory_space=pl.ANY)


def place(z, y, core):
    return ((z % NZ) * NY + y % NY) * NC + core


def send(x, move):
    route = []
    for b in range(BLK):
        z, y, core = b // (NY * NC), b // NC % NY, b % NC
        for r in range(NR):
            z2, y2, core2, r2 = move(z, y, core, r)
            route.append((b * NR + r, place(z2, y2, core2) * NR + r2 % NR))
    return lax.ppermute(x, ("blk", "rep"), route)


def to_core(z, y, core, r):
    return z, y, 1 - core, r


def to_row(z, y, core, r):
    if core == 0:
        dz, to = ((1, 1), (0, 0), (2, 2), (-1, 3))[r]
    else:
        dz, to = ((1, 0), (2, 1), (0, 3), (-1, 2))[r]
    return z + dz, y, core, to


def along(steps):
    def move(z, y, core, r):
        if core == 0:
            return z, y + steps, core, r if y + steps < NY else r - 1
        return z, y - steps, core, r if y >= steps else r + 1

    return move


def send_y(x, s):
    return send(x, lambda z, y, core, r: (z, y + s, core, r))


def send_z(x, s):
    return send(x, lambda z, y, core, r: (z + s, y, core, r))


def send_rep(x, s):
    return lax.ppermute(x, "rep", [(r, (r + s) % NR) for r in range(NR)])


def send_col(x):
    return lax.ppermute(x, "col", [(0, 1), (1, 0)])


def sds(shape, dtype):
    return jax.ShapeDtypeStruct(shape, dtype)


def params(mib=40):
    return pltpu.CompilerParams(vmem_limit_bytes=mib << 20)


def cost(flops, nbytes):
    return pl.CostEstimate(flops=flops, bytes_accessed=nbytes, transcendentals=0)


def prep_kernel(ids, g, deg, keep, give):
    flip = ids[0] == 1
    for t in range(NT):
        scale = 1.0 / deg[pl.ds(t, 1), :].astype(F32)
        turned = (jnp.transpose(g[t].astype(F32)) * scale).astype(BF)
        low, high = turned[:HALF], turned[HALF:]
        keep[t] = jnp.where(flip, high, low)
        give[t] = jnp.where(flip, low, high)


def prep(ids, g, deg):
    half = sds((NT, HALF, TILE), BF)
    return pl.pallas_call(
        prep_kernel,
        out_shape=(half, half),
        in_specs=[SMEM, VMEM, VMEM],
        out_specs=(VMEM, VMEM),
        compiler_params=params(8),
        cost_estimate=cost(1 << 20, 1 << 20),
        name="prep",
    )(ids, g, deg)


GROUP = 4


def spmm_kernel(items, last, plan, rows, cols, counts, tv, *refs):
    n = len(items)
    arrays = 2 * (1 + max(k for k, _ in items))
    sources, refs = refs[:arrays], refs[arrays:]
    if last:
        before, own, *outs, acc = refs
        acc[pl.ds(0, NT)] = before[...]
    else:
        after, acc = refs
        acc[...] = jnp.zeros_like(acc)
    slots = tv.shape[1]
    for i, (k, parity) in enumerate(items):
        mine, theirs = sources[2 * k], sources[2 * k + 1]
        j = jnp.maximum(plan[i], 0)
        live = jnp.where(plan[i] >= 0, jnp.clip(counts[0, j], 0, slots), 0)

        @pl.loop(0, (live + (GROUP - 1)) >> 2)
        def _(g, j=j, live=live, mine=mine, theirs=theirs, parity=parity):
            products, targets = [], []
            for u in range(GROUP):
                t = g * GROUP + u
                row = rows[j, t]
                source = jnp.concatenate([mine[parity, row], theirs[1 - parity, row]], axis=0)
                products.append(jnp.dot(source, tv[j, t], preferred_element_type=F32))
                targets.append(jnp.where(t < live, cols[j, t], NT))
            for target, product in zip(targets, products):
                acc[target] += product

    if last:
        me = plan[n]
        q = NT // NR
        for i in range(q):
            own[i] = acc[me * q + i]
            for s in range(1, NR):
                to = (me + s) % NR
                outs[s - 1][i] = acc[to * q + i].astype(BF)
    else:
        after[...] = acc[pl.ds(0, NT)]


def spmm(plan, tables, tv, items, pairs, before=None):
    last = before is not None
    flat = [x for pair in pairs for x in pair]
    q = NT // NR
    if last:
        out_shape = (sds((q, TILE, TILE), F32),) + (sds((q, TILE, TILE), BF),) * 3
        out_specs = (VMEM,) * 4
    else:
        out_shape, out_specs = sds((NT, TILE, TILE), F32), VMEM
    return pl.pallas_call(
        functools.partial(spmm_kernel, items, last),
        out_shape=out_shape,
        in_specs=[SMEM] * 4 + [VMEM] * (1 + len(flat) + last),
        out_specs=out_specs,
        scratch_shapes=[pltpu.VMEM((NT + 1, TILE, TILE), F32)],
        compiler_params=params(20),
        cost_estimate=cost(len(items) * 10 * 2 * TILE**3, len(items) << 20),
        name="tiles",
    )(plan, *tables, tv, *flat, *([before] if last else []))


def finish_kernel(mine, theirs, wn, self_term, out):
    for t in range(NT // NR):
        y = jnp.concatenate([mine[t], theirs[t]], axis=0)
        turned = jnp.dot(wn[...], y, preferred_element_type=F32)
        rows = pl.ds(t * TILE, TILE)
        out[rows, :] = (self_term[rows, :] + jnp.transpose(turned)).astype(BF)


def finish(mine, theirs, wn, self_term):
    return pl.pallas_call(
        finish_kernel,
        out_shape=sds(self_term.shape, BF),
        in_specs=[VMEM] * 4,
        out_specs=VMEM,
        compiler_params=params(8),
        cost_estimate=cost(2 * 512 * 256 * 128, 1 << 19),
        name="finish",
    )(mine, theirs, wn, self_term)


def in_order(parts, me, axis):
    n = len(parts)
    slots = jnp.stack(parts[::-1] * 2)
    at = (n - 1 - me) % n
    return jnp.concatenate(
        [
            lax.dynamic_index_in_dim(slots, at + i, 0, keepdims=False)
            for i in range(n)
        ],
        axis=axis,
    )


def reduce_pieces(x, me, move, n):
    total = lax.dynamic_index_in_dim(x, me, 0, keepdims=False)
    for s in range(1, n):
        total = total + move(
            lax.dynamic_index_in_dim(x, (me + s) % n, 0, keepdims=False), s
        )
    return total


def weight_sum(partial, y, rep):
    by_rep = partial.reshape(2, NR, -1, 256).transpose(1, 0, 2, 3)
    mine = reduce_pieces(by_rep, rep, send_rep, NR)
    by_y = mine.reshape(2, NY, -1, 256).transpose(1, 0, 2, 3)
    mine = reduce_pieces(by_y, y, send_y, NY)
    mine = mine + sum(send_z(mine, s) for s in range(1, NZ))
    mine = mine + send(mine, to_core)
    mine = in_order([mine] + [send_y(mine, s) for s in range(1, NY)], y, 1)
    return in_order([mine] + [send_rep(mine, s) for s in range(1, NR)], rep, 1)


def shards(
    feats, agg_feats, grad_out, w_self, w_neigh, degree, tile_vals, tile_rows, tile_cols, tile_count
):
    blk, rep, col = (lax.axis_index(a) for a in ("blk", "rep", "col"))
    core, y = blk % NC, blk // NC % NY
    ids = jnp.stack([core, y, rep]).astype(jnp.int32)
    row_count, width = feats.shape
    quarter = row_count // NR
    tables = (tile_rows[0], tile_cols[0], tile_count)
    tv = tile_vals[0]

    keep, give = prep(ids, grad_out.reshape(NT, TILE, width), degree.reshape(NT, TILE))
    held = jnp.stack([keep, send(give, to_core)])
    near = send(held, to_row)
    step1 = send(near, along(1))
    step3 = send(near, along(3))
    far = send(near, lambda z, y, core, r: (z, y, core, r - 1 if core == 0 else r + 1))
    step2 = send(step1, along(1))
    near_x, step1_x, step3_x, far_x, step2_x = (
        send(x, to_core) for x in (near, step1, step3, far, step2)
    )
    pairs = [(near, far_x), (step1, step3_x), (step3, step1_x), (far, near_x)]
    outer = [((0, 0), 0, -1), ((3, 0), -1, 0), ((3, 1), 7, 1)]
    outer += [((1, 0), 2, 6), ((1, 1), 1, 7), ((2, 0), 6, 2), ((2, 1), 5, 3)]
    inner = [((0, 0), 4, 4), ((0, 1), 3, 5)]
    plan = lambda table: [jnp.where(core == 0, a, b) for _, a, b in table]
    acc = spmm(jnp.stack(plan(outer)), tables, tv, [i for i, _, _ in outer], pairs)
    own, *outs = spmm(
        jnp.stack(plan(inner) + [rep]), tables, tv, [i for i, _, _ in inner], [(step2, step2_x)], acc
    )
    total = own
    for shift, piece in enumerate(outs, 1):
        total = total + send_rep(piece, shift).astype(F32)
    mine = total.astype(BF)

    rows = lambda x: lax.dynamic_slice_in_dim(x, rep * quarter, quarter, 0)
    g_own = rows(grad_out)
    g_other = send_col(g_own)
    g_rows = jnp.where(
        col == 0,
        jnp.concatenate([g_own, g_other], axis=1),
        jnp.concatenate([g_other, g_own], axis=1),
    )
    self_term = lax.dot_general(
        g_rows, w_self, (((1,), (1,)), ((), ())), preferred_element_type=F32
    )
    over_rows = (((0,), (0,)), ((), ()))
    partial = jnp.stack(
        [
            lax.dot_general(rows(x), g_rows, over_rows, preferred_element_type=F32)
            for x in (feats, agg_feats)
        ]
    )
    node_count = row_count * lax.axis_size("blk")
    grad_weight = weight_sum(partial, y, rep) * (1.0 / math.sqrt(node_count))

    own_first = [jnp.where(col == 0, w_neigh[:, i : i + HALF], w_neigh[:, width + i : width + i + HALF]) for i in (0, HALF)]
    other = [jnp.where(col == 0, w_neigh[:, width + i : width + i + HALF], w_neigh[:, i : i + HALF]) for i in (0, HALF)]
    turn = lambda pair: [jnp.where(core == 0, *pair), jnp.where(core == 0, *pair[::-1])]
    wn = jnp.concatenate(turn(own_first) + turn(other), axis=1)
    block = finish(mine, send_col(mine), wn, self_term)
    grad_feats = in_order([block] + [send_rep(block, s) for s in range(1, NR)], rep, 0)
    return (grad_feats, grad_weight)


def solution(mesh):
    placed = (
        P("blk", "col"),
        P("blk", "col"),
        P("blk", "col"),
        P("col", None),
        P("col", None),
        P("blk"),
        P("blk", "rep", None, None, None),
        P("blk", "rep", None),
        P("blk", "rep", None),
        P("blk", "rep"),
    )
    return jax.shard_map(
        shards,
        mesh=mesh,
        in_specs=placed,
        out_specs=(P("blk", "col"), P(None, "col", None)),
        check_vma=False,
    )
```

```python
import functools
import math

import jax
import jax.numpy as jnp
from jax import lax
from jax.experimental import pallas as pl
from jax.experimental.pallas import tpu as pltpu
from jax.sharding import PartitionSpec as P

NZ, NY, NC, NR = 4, 4, 2, 4
BLK = NZ * NY * NC
TILE = 128
NT = 16
HALF = 64
BF = jnp.bfloat16
F32 = jnp.float32
VMEM = pl.BlockSpec(memory_space=pltpu.VMEM)
SMEM = pl.BlockSpec(memory_space=pltpu.SMEM)
HBM = pl.BlockSpec(memory_space=pltpu.HBM)


def place(z, y, core):
    return ((z % NZ) * NY + y % NY) * NC + core


def send(x, move):
    route = []
    for b in range(BLK):
        z, y, core = b // (NY * NC), b // NC % NY, b % NC
        for r in range(NR):
            z2, y2, core2, r2 = move(z, y, core, r)
            route.append((b * NR + r, place(z2, y2, core2) * NR + r2 % NR))
    return lax.ppermute(x, ("blk", "rep"), route)


def to_core(z, y, core, r):
    return z, y, 1 - core, r


def to_row(z, y, core, r):
    if core == 0:
        dz, to = ((1, 1), (0, 0), (2, 2), (-1, 3))[r]
    else:
        dz, to = ((1, 0), (2, 1), (0, 3), (-1, 2))[r]
    return z + dz, y, core, to


def along(steps):
    def move(z, y, core, r):
        if core == 0:
            return z, y + steps, core, r if y + steps < NY else r - 1
        return z, y - steps, core, r if y >= steps else r + 1

    return move


def send_rep(x, s):
    return lax.ppermute(x, "rep", [(r, (r + s) % NR) for r in range(NR)])


def send_col(x):
    return lax.ppermute(x, "col", [(0, 1), (1, 0)])


def sds(shape, dtype):
    return jax.ShapeDtypeStruct(shape, dtype)


def params(mib=40):
    return pltpu.CompilerParams(vmem_limit_bytes=mib << 20)


def cost(flops, nbytes):
    return pl.CostEstimate(flops=flops, bytes_accessed=nbytes, transcendentals=0)


PARTS = 4


def prep_kernel(ids, g, deg, keep, give, g_buf, deg_buf, sems):
    flip = ids[0] == 1
    count = NT // PARTS
    copies = [
        pltpu.make_async_copy(
            g.at[pl.ds(i * count, count)], g_buf.at[pl.ds(i * count, count)], sems.at[i]
        )
        for i in range(PARTS)
    ]
    copies.insert(0, pltpu.make_async_copy(deg, deg_buf, sems.at[PARTS]))
    for c in copies:
        c.start()
    copies[0].wait()
    for t in range(NT):
        if t % count == 0:
            copies[1 + t // count].wait()
        scale = 1.0 / deg_buf[pl.ds(t, 1), :].astype(F32)
        turned = (jnp.transpose(g_buf[t].astype(F32)) * scale).astype(BF)
        low, high = turned[:HALF], turned[HALF:]
        keep[t] = jnp.where(flip, high, low)
        give[t] = jnp.where(flip, low, high)


def prep(ids, g, deg):
    half = sds((NT, HALF, TILE), BF)
    g, deg = (pltpu.with_memory_space_constraint(x, pltpu.HBM) for x in (g, deg))
    return pl.pallas_call(
        prep_kernel,
        out_shape=(half, half),
        in_specs=[SMEM, HBM, HBM],
        out_specs=(VMEM, VMEM),
        scratch_shapes=[
            pltpu.VMEM((NT, TILE, TILE), BF),
            pltpu.VMEM((NT, TILE), jnp.int32),
            pltpu.SemaphoreType.DMA((PARTS + 1,)),
        ],
        compiler_params=params(8),
        cost_estimate=cost(1 << 20, 1 << 20),
        name="prep",
    )(ids, g, deg)


GROUP = 4


def spmm_kernel(items, last, base, table, tv, *refs):
    n = len(items)
    arrays = 2 * (1 + max(k for k, _ in items))
    sources, refs = refs[:arrays], refs[arrays:]
    *refs, acc, tiles, sems = refs
    distances, slots = tv.shape[1:3]
    plan = [table[distances, base + i] for i in range(n)]
    which = [jnp.maximum(p, 0) for p in plan]
    live = [jnp.where(p >= 0, jnp.clip(table[w, 2 * slots], 0, slots), 0) for p, w in zip(plan, which)]
    groups = [(x + (GROUP - 1)) >> 2 for x in live]

    def copy(i, g):
        part = pl.ds(g * GROUP, GROUP)
        return pltpu.make_async_copy(tv.at[0, which[i], part], tiles.at[i, part], sems.at[i, g])

    for i in range(n):

        @pl.loop(0, groups[i])
        def _(g, i=i):
            copy(i, g).start()

    if last:
        before, own, *outs = refs
        acc[pl.ds(0, NT)] = before[...]
    else:
        (result,) = refs
        acc[...] = jnp.zeros_like(acc)
    for i, (k, parity) in enumerate(items):
        mine, theirs = sources[2 * k], sources[2 * k + 1]

        @pl.loop(0, groups[i])
        def _(g, i=i, mine=mine, theirs=theirs, parity=parity):
            copy(i, g).wait()
            products, targets = [], []
            for u in range(GROUP):
                t = g * GROUP + u
                row = table[which[i], t]
                source = jnp.concatenate([mine[parity, row], theirs[1 - parity, row]], axis=0)
                products.append(jnp.dot(source, tiles[i, t], preferred_element_type=F32))
                targets.append(jnp.where(t < live[i], table[which[i], slots + t], NT))
            for target, product in zip(targets, products):
                acc[target] += product

    if last:
        me = table[distances, 0]
        q = NT // NR
        for i in range(q):
            own[i] = acc[me * q + i]
            for s in range(1, NR):
                to = (me + s) % NR
                outs[s - 1][i] = acc[to * q + i].astype(BF)
    else:
        result[...] = acc[pl.ds(0, NT)]


def spmm(table, base, tv, items, pairs, *more):
    last = len(more) > 0
    flat = [x for pair in pairs for x in pair]
    q, n, slots = NT // NR, len(items), tv.shape[2]
    if last:
        out_shape = (sds((q, TILE, TILE), F32),) + (sds((q, TILE, TILE), BF),) * 3
        out_specs = (VMEM,) * 4
    else:
        out_shape, out_specs = sds((NT, TILE, TILE), F32), VMEM
    return pl.pallas_call(
        functools.partial(spmm_kernel, items, last, base),
        out_shape=out_shape,
        in_specs=[SMEM, HBM] + [VMEM] * (len(flat) + len(more)),
        out_specs=out_specs,
        scratch_shapes=[
            pltpu.VMEM((NT + 1, TILE, TILE), F32),
            pltpu.VMEM((n, slots, TILE, TILE), BF),
            pltpu.SemaphoreType.DMA((n, slots // GROUP)),
        ],
        compiler_params=params(4 + 4 * n // 3),
        cost_estimate=cost(n * 10 * 2 * TILE**3, n << 20),
        name="tiles",
    )(table, tv, *flat, *more)


def finish_kernel(scale, mine, theirs, wn, self_term, extra, out):
    out[pl.ds(self_term.shape[0], TILE), :] = (extra[...] * scale).astype(BF)
    for t in range(NT // NR):
        y = jnp.concatenate([mine[t], theirs[t]], axis=0)
        turned = jnp.dot(wn[...], y, preferred_element_type=F32)
        rows = pl.ds(t * TILE, TILE)
        out[rows, :] = (self_term[rows, :] + jnp.transpose(turned)).astype(BF)


def finish(mine, theirs, wn, self_term, extra, scale):
    return pl.pallas_call(
        functools.partial(finish_kernel, scale),
        out_shape=sds((self_term.shape[0] + TILE, TILE), BF),
        in_specs=[VMEM] * 5,
        out_specs=VMEM,
        compiler_params=params(8),
        cost_estimate=cost(2 * 512 * 256 * 128, 1 << 19),
        name="finish",
    )(mine, theirs, wn, self_term, extra)


def in_order(parts, me, axis):
    n = len(parts)
    slots = jnp.stack(parts[::-1] * 2)
    at = (n - 1 - me) % n
    return jnp.concatenate(
        [
            lax.dynamic_index_in_dim(slots, at + i, 0, keepdims=False)
            for i in range(n)
        ],
        axis=axis,
    )


def after(x, *others):
    return lax.optimization_barrier((x,) + others)[0]


def sum_four(x, axis, mark):
    if axis == "y":
        got = [send(x, lambda z, y, core, r, m=m: (z, y ^ m, core, r)) for m in (1, 2, 3)]
    else:
        got = [send(x, lambda z, y, core, r, m=m: (z ^ m, y, core, r)) for m in (1, 2, 3)]
    got = lax.optimization_barrier((*got, mark))
    return (x + got[0]) + (got[1] + got[2])


def shards(
    feats, agg_feats, grad_out, w_self, w_neigh, degree, tile_vals, tile_rows, tile_cols, tile_count
):
    blk, rep, col = (lax.axis_index(a) for a in ("blk", "rep", "col"))
    core = blk % NC
    ids = jnp.stack([core, rep]).astype(jnp.int32)
    row_count, width = feats.shape
    quarter = row_count // NR

    keep, give = prep(ids, grad_out.reshape(NT, TILE, width), degree.reshape(NT, TILE))
    held = jnp.stack([keep, send(give, to_core)])
    near = send(held, to_row)
    tv = pltpu.with_memory_space_constraint(tile_vals, pltpu.HBM)
    outer = [((0, 0), 0, -1), ((3, 0), -1, 0), ((3, 1), 7, 1)]
    outer += [((1, 0), 2, 6), ((1, 1), 1, 7), ((2, 0), 6, 2), ((2, 1), 5, 3)]
    inner = [((0, 0), 4, 4), ((0, 1), 3, 5)]
    at = [rep] + [jnp.where(core == 0, a, b) for _, a, b in outer + inner]
    table = jnp.concatenate([tile_rows[0], tile_cols[0], tile_count.reshape(-1, 1)], axis=1)
    plan = jnp.pad(jnp.stack(at).astype(jnp.int32), (0, table.shape[1] - len(at)))
    table = after(jnp.concatenate([table, plan[None]], axis=0), held)
    own_first = [jnp.where(col == 0, w_neigh[:, i : i + HALF], w_neigh[:, width + i : width + i + HALF]) for i in (0, HALF)]
    other = [jnp.where(col == 0, w_neigh[:, width + i : width + i + HALF], w_neigh[:, i : i + HALF]) for i in (0, HALF)]
    turn = lambda pair: [jnp.where(core == 0, *pair), jnp.where(core == 0, *pair[::-1])]
    wn = jnp.concatenate(turn(own_first) + turn(other), axis=1)
    rows = lambda x: lax.dynamic_slice_in_dim(x, rep * quarter, quarter, 0)
    g_own = after(rows(grad_out), held)
    near, table, wn, g_own = lax.optimization_barrier((near, table, wn, g_own))
    step1 = send(near, along(1))
    step3 = send(near, along(3))
    far = send(near, lambda z, y, core, r: (z, y, core, r - 1 if core == 0 else r + 1))
    step2 = send(step1, along(1))
    near_x, step1_x, step3_x, far_x = (send(x, to_core) for x in (near, step1, step3, far))
    pairs = [(near, far_x), (step1, step3_x), (step3, step1_x), (far, near_x)]
    items = lambda plan: [i for i, _, _ in plan]
    g_other = send_col(g_own)
    g_other = after(g_other, step1, step3, far)
    g_rows = jnp.where(
        col == 0,
        jnp.concatenate([g_own, g_other], axis=1),
        jnp.concatenate([g_other, g_own], axis=1),
    )
    self_term = lax.dot_general(
        g_rows, w_self, (((1,), (1,)), ((), ())), preferred_element_type=F32
    )
    over_rows = (((0,), (0,)), ((), ()))
    partial = jnp.stack(
        [
            lax.dot_general(rows(x), g_rows, over_rows, preferred_element_type=F32)
            for x in (feats, agg_feats)
        ]
    )
    rows_each = partial.shape[1] // NR
    for_rep = lambda s: lax.dynamic_slice_in_dim(partial, (rep + s) % NR * rows_each, rows_each, 1)
    step2, *parts = lax.optimization_barrier((step2, *(for_rep(s) for s in range(NR))))
    step2_x = send(step2, to_core)
    acc = spmm(table, 1, tv, items(outer), pairs)
    got = [send_rep(parts[s], s) for s in range(1, NR)]
    piece = parts[0] + sum(lax.optimization_barrier((*got, acc))[:-1])
    piece = piece + send(piece, to_core)

    own, *outs = spmm(table, 1 + len(outer), tv, items(inner), [(step2, step2_x)], acc)
    total = own + sum(send_rep(x, s).astype(F32) for s, x in enumerate(outs, 1))
    mine = total.astype(BF)
    theirs = send_col(mine)
    piece = sum_four(after(piece, own), "z", mine)
    piece = sum_four(piece, "y", theirs).reshape(TILE, TILE)
    scale = 1.0 / math.sqrt(row_count * lax.axis_size("blk"))
    block = finish(mine, theirs, wn, self_term, piece, scale)
    blocks = [block] + [send_rep(block, s) for s in range(1, NR)]
    grad_feats = in_order([x[:quarter] for x in blocks], rep, 0)
    pieces = [x[quarter:].reshape(2, -1, 256).astype(F32) for x in blocks]
    return (grad_feats, in_order(pieces, rep, 1))


def solution(mesh):
    placed = (
        P("blk", "col"),
        P("blk", "col"),
        P("blk", "col"),
        P("col", None),
        P("col", None),
        P("blk"),
        P("blk", "rep", None, None, None),
        P("blk", "rep", None),
        P("blk", "rep", None),
        P("blk", "rep"),
    )
    return jax.shard_map(
        shards,
        mesh=mesh,
        in_specs=placed,
        out_specs=(P("blk", "col"), P(None, "col", None)),
        check_vma=False,
    )
```

```python
import functools
import math

import jax
import jax.numpy as jnp
from jax import lax
from jax.experimental import pallas as pl
from jax.experimental.pallas import tpu as pltpu
from jax.sharding import PartitionSpec as P

NZ, NY, NC, NR = 4, 4, 2, 4
BLK = NZ * NY * NC
TILE = 128
NT = 16
HALF = 64
BF = jnp.bfloat16
F32 = jnp.float32
VMEM = pl.BlockSpec(memory_space=pltpu.VMEM)
SMEM = pl.BlockSpec(memory_space=pltpu.SMEM)
HBM = pl.BlockSpec(memory_space=pltpu.HBM)


def place(z, y, core):
    return ((z % NZ) * NY + y % NY) * NC + core


def send(x, move):
    route = []
    for b in range(BLK):
        z, y, core = b // (NY * NC), b // NC % NY, b % NC
        for r in range(NR):
            z2, y2, core2, r2 = move(z, y, core, r)
            route.append((b * NR + r, place(z2, y2, core2) * NR + r2 % NR))
    return lax.ppermute(x, ("blk", "rep"), route)


def to_core(z, y, core, r):
    return z, y, 1 - core, r


def to_row(z, y, core, r):
    if core == 0:
        dz, to = ((1, 1), (0, 0), (2, 2), (-1, 3))[r]
    else:
        dz, to = ((1, 0), (2, 1), (0, 3), (-1, 2))[r]
    return z + dz, y, core, to


def along(steps):
    def move(z, y, core, r):
        if core == 0:
            return z, y + steps, core, r if y + steps < NY else r - 1
        return z, y - steps, core, r if y >= steps else r + 1

    return move


def send_rep(x, s):
    return lax.ppermute(x, "rep", [(r, (r + s) % NR) for r in range(NR)])


def send_col(x):
    return lax.ppermute(x, "col", [(0, 1), (1, 0)])


def sds(shape, dtype):
    return jax.ShapeDtypeStruct(shape, dtype)


def params(mib=40):
    return pltpu.CompilerParams(vmem_limit_bytes=mib << 20)


def cost(flops, nbytes):
    return pl.CostEstimate(flops=flops, bytes_accessed=nbytes, transcendentals=0)


PARTS = 4


def prep_kernel(ids, g, deg, keep, give, g_buf, deg_buf, sems):
    flip = ids[0] == 1
    count = NT // PARTS
    copies = [
        pltpu.make_async_copy(
            g.at[pl.ds(i * count, count)], g_buf.at[pl.ds(i * count, count)], sems.at[i]
        )
        for i in range(PARTS)
    ]
    copies.insert(0, pltpu.make_async_copy(deg, deg_buf, sems.at[PARTS]))
    for c in copies:
        c.start()
    copies[0].wait()
    for t in range(NT):
        if t % count == 0:
            copies[1 + t // count].wait()
        scale = 1.0 / deg_buf[pl.ds(t, 1), :].astype(F32)
        turned = (jnp.transpose(g_buf[t].astype(F32)) * scale).astype(BF)
        low, high = turned[:HALF], turned[HALF:]
        keep[t] = jnp.where(flip, high, low)
        give[t] = jnp.where(flip, low, high)


def prep(ids, g, deg):
    half = sds((NT, HALF, TILE), BF)
    g, deg = (pltpu.with_memory_space_constraint(x, pltpu.HBM) for x in (g, deg))
    return pl.pallas_call(
        prep_kernel,
        out_shape=(half, half),
        in_specs=[SMEM, HBM, HBM],
        out_specs=(VMEM, VMEM),
        scratch_shapes=[
            pltpu.VMEM((NT, TILE, TILE), BF),
            pltpu.VMEM((NT, TILE), jnp.int32),
            pltpu.SemaphoreType.DMA((PARTS + 1,)),
        ],
        compiler_params=params(8),
        cost_estimate=cost(1 << 20, 1 << 20),
        name="prep",
    )(ids, g, deg)


GROUP = 4


def spmm_kernel(items, last, base, table, tv, *refs):
    n = len(items)
    arrays = 2 * (1 + max(k for k, _ in items))
    sources, refs = refs[:arrays], refs[arrays:]
    *refs, acc, tiles, sems = refs
    distances, slots = tv.shape[1:3]
    plan = [table[distances, base + i] for i in range(n)]
    which = [jnp.maximum(p, 0) for p in plan]
    live = [jnp.where(p >= 0, jnp.clip(table[w, 2 * slots], 0, slots), 0) for p, w in zip(plan, which)]
    groups = [(x + (GROUP - 1)) >> 2 for x in live]

    def copy(i, g):
        part = pl.ds(g * GROUP, GROUP)
        return pltpu.make_async_copy(tv.at[0, which[i], part], tiles.at[i, part], sems.at[i, g])

    for i in range(n):

        @pl.loop(0, groups[i])
        def _(g, i=i):
            copy(i, g).start()

    if last:
        before, own, *outs = refs
        acc[pl.ds(0, NT)] = before[...]
    else:
        (result,) = refs
        acc[...] = jnp.zeros_like(acc)
    for i, (k, parity) in enumerate(items):
        mine, theirs = sources[2 * k], sources[2 * k + 1]

        @pl.loop(0, groups[i])
        def _(g, i=i, mine=mine, theirs=theirs, parity=parity):
            copy(i, g).wait()
            products, targets = [], []
            for u in range(GROUP):
                t = g * GROUP + u
                row = table[which[i], t]
                source = jnp.concatenate([mine[parity, row], theirs[1 - parity, row]], axis=0)
                products.append(jnp.dot(source, tiles[i, t], preferred_element_type=F32))
                targets.append(jnp.where(t < live[i], table[which[i], slots + t], NT))
            for target, product in zip(targets, products):
                acc[target] += product

    if last:
        me = table[distances, 0]
        q = NT // NR
        for i in range(q):
            own[i] = acc[me * q + i]
            for s in range(1, NR):
                to = (me + s) % NR
                outs[s - 1][i] = acc[to * q + i].astype(BF)
    else:
        result[...] = acc[pl.ds(0, NT)]


def spmm(table, base, tv, items, pairs, *more):
    last = len(more) > 0
    flat = [x for pair in pairs for x in pair]
    q, n, slots = NT // NR, len(items), tv.shape[2]
    if last:
        out_shape = (sds((q, TILE, TILE), F32),) + (sds((q, TILE, TILE), BF),) * 3
        out_specs = (VMEM,) * 4
    else:
        out_shape, out_specs = sds((NT, TILE, TILE), F32), VMEM
    return pl.pallas_call(
        functools.partial(spmm_kernel, items, last, base),
        out_shape=out_shape,
        in_specs=[SMEM, HBM] + [VMEM] * (len(flat) + len(more)),
        out_specs=out_specs,
        scratch_shapes=[
            pltpu.VMEM((NT + 1, TILE, TILE), F32),
            pltpu.VMEM((n, slots, TILE, TILE), BF),
            pltpu.SemaphoreType.DMA((n, slots // GROUP)),
        ],
        compiler_params=params(4 + 4 * n // 3),
        cost_estimate=cost(n * 10 * 2 * TILE**3, n << 20),
        name="tiles",
    )(table, tv, *flat, *more)


def finish_kernel(scale, mine, theirs, wn, self_term, extra, out):
    out[pl.ds(self_term.shape[0], TILE), :] = (extra[...] * scale).astype(BF)
    for t in range(NT // NR):
        y = jnp.concatenate([mine[t], theirs[t]], axis=0)
        turned = jnp.dot(wn[...], y, preferred_element_type=F32)
        rows = pl.ds(t * TILE, TILE)
        out[rows, :] = (self_term[rows, :] + jnp.transpose(turned)).astype(BF)


def finish(mine, theirs, wn, self_term, extra, scale):
    return pl.pallas_call(
        functools.partial(finish_kernel, scale),
        out_shape=sds((self_term.shape[0] + TILE, TILE), BF),
        in_specs=[VMEM] * 5,
        out_specs=VMEM,
        compiler_params=params(8),
        cost_estimate=cost(2 * 512 * 256 * 128, 1 << 19),
        name="finish",
    )(mine, theirs, wn, self_term, extra)


def in_order(parts, me, axis):
    n = len(parts)
    slots = jnp.stack(parts[::-1] * 2)
    at = (n - 1 - me) % n
    return jnp.concatenate(
        [
            lax.dynamic_index_in_dim(slots, at + i, 0, keepdims=False)
            for i in range(n)
        ],
        axis=axis,
    )


def after(x, *others):
    return lax.optimization_barrier((x,) + others)[0]


def sum_four(x, axis, mark):
    if axis == "y":
        got = [send(x, lambda z, y, core, r, m=m: (z, y ^ m, core, r)) for m in (1, 2, 3)]
    else:
        got = [send(x, lambda z, y, core, r, m=m: (z ^ m, y, core, r)) for m in (1, 2, 3)]
    got = lax.optimization_barrier((*got, mark))
    return (x + got[0]) + (got[1] + got[2])


def shards(
    feats, agg_feats, grad_out, w_self, w_neigh, degree, tile_vals, tile_rows, tile_cols, tile_count
):
    blk, rep, col = (lax.axis_index(a) for a in ("blk", "rep", "col"))
    core = blk % NC
    ids = jnp.stack([core, rep]).astype(jnp.int32)
    row_count, width = feats.shape
    quarter = row_count // NR

    keep, give = prep(ids, grad_out.reshape(NT, TILE, width), degree.reshape(NT, TILE))
    held = jnp.stack([keep, send(give, to_core)])
    near = send(held, to_row)
    tv = pltpu.with_memory_space_constraint(tile_vals, pltpu.HBM)
    outer = [((0, 0), 0, -1), ((3, 0), -1, 0), ((3, 1), 7, 1)]
    outer += [((1, 0), 2, 6), ((1, 1), 1, 7), ((2, 0), 6, 2), ((2, 1), 5, 3)]
    inner = [((0, 0), 4, 4), ((0, 1), 3, 5)]
    at = [rep] + [jnp.where(core == 0, a, b) for _, a, b in outer + inner]
    table = jnp.concatenate([tile_rows[0], tile_cols[0], tile_count.reshape(-1, 1)], axis=1)
    plan = jnp.pad(jnp.stack(at).astype(jnp.int32), (0, table.shape[1] - len(at)))
    table = after(jnp.concatenate([table, plan[None]], axis=0), held)
    own_first = [jnp.where(col == 0, w_neigh[:, i : i + HALF], w_neigh[:, width + i : width + i + HALF]) for i in (0, HALF)]
    other = [jnp.where(col == 0, w_neigh[:, width + i : width + i + HALF], w_neigh[:, i : i + HALF]) for i in (0, HALF)]
    turn = lambda pair: [jnp.where(core == 0, *pair), jnp.where(core == 0, *pair[::-1])]
    wn = jnp.concatenate(turn(own_first) + turn(other), axis=1)
    rows = lambda x: lax.dynamic_slice_in_dim(x, rep * quarter, quarter, 0)
    g_own = after(rows(grad_out), held)
    near, table, wn, g_own = lax.optimization_barrier((near, table, wn, g_own))
    step1 = send(near, along(1))
    step3 = send(near, along(3))
    far = send(near, lambda z, y, core, r: (z, y, core, r - 1 if core == 0 else r + 1))
    step2 = send(step1, along(1))
    items = lambda plan: [i for i, _, _ in plan]
    g_other = send_col(g_own)
    g_other = after(g_other, step1, step3, far)
    g_rows = jnp.where(
        col == 0,
        jnp.concatenate([g_own, g_other], axis=1),
        jnp.concatenate([g_other, g_own], axis=1),
    )
    self_term = lax.dot_general(
        g_rows, w_self, (((1,), (1,)), ((), ())), preferred_element_type=F32
    )
    over_rows = (((0,), (0,)), ((), ()))
    partial = jnp.stack(
        [
            lax.dot_general(rows(x), g_rows, over_rows, preferred_element_type=F32)
            for x in (feats, agg_feats)
        ]
    )
    rows_each = partial.shape[1] // NR
    for_rep = lambda s: lax.dynamic_slice_in_dim(partial, (rep + s) % NR * rows_each, rows_each, 1)
    parts = [for_rep(s) for s in range(NR)]
    step1, step3, far, *parts = lax.optimization_barrier((step1, step3, far, *parts))
    near_x, step1_x, step3_x, far_x, step2_x = (
        send(x, to_core) for x in (near, step1, step3, far, step2)
    )
    pairs = [(near, far_x), (step1, step3_x), (step3, step1_x), (far, near_x)]
    acc = spmm(table, 1, tv, items(outer), pairs)
    got = [send_rep(parts[s], s) for s in range(1, NR)]
    piece = parts[0] + sum(lax.optimization_barrier((*got, acc))[:-1])
    piece = piece + send(piece, to_core)

    own, *outs = spmm(table, 1 + len(outer), tv, items(inner), [(step2, step2_x)], acc)
    total = own + sum(send_rep(x, s).astype(F32) for s, x in enumerate(outs, 1))
    mine = total.astype(BF)
    theirs = send_col(mine)
    piece = sum_four(after(piece, own), "y", mine)
    piece = sum_four(after(piece, theirs), "z", theirs).reshape(TILE, TILE)
    scale = 1.0 / math.sqrt(row_count * lax.axis_size("blk"))
    block = finish(mine, theirs, wn, self_term, piece, scale)
    blocks = [block] + [send_rep(block, s) for s in range(1, NR)]
    grad_feats = in_order([x[:quarter] for x in blocks], rep, 0)
    pieces = [x[quarter:].reshape(2, -1, 256).astype(F32) for x in blocks]
    return (grad_feats, in_order(pieces, rep, 1))


def solution(mesh):
    placed = (
        P("blk", "col"),
        P("blk", "col"),
        P("blk", "col"),
        P("col", None),
        P("col", None),
        P("blk"),
        P("blk", "rep", None, None, None),
        P("blk", "rep", None),
        P("blk", "rep", None),
        P("blk", "rep"),
    )
    return jax.shard_map(
        shards,
        mesh=mesh,
        in_specs=placed,
        out_specs=(P("blk", "col"), P(None, "col", None)),
        check_vma=False,
    )
```
